256 devices in a mesh: pole: 16 (over z, x_hi), lat: 4 (over x_lo, core), lon: 4 (over y).
Axes of the slice: x: 4 (x_hi: 2, x_lo: 2; x = x_hi * 2 + x_lo), y: 4, z: 8, core: 2. Of those that a mesh axis runs over, the one named last changes fastest.
Arguments:
- height: float32 [512, 4096], P(('lat', 'pole'), 'lon'), may hold values from -6 to 6
- east_wind: float32 [512, 4096], P(('lat', 'pole'), 'lon'), may hold values from -6 to 6
- north_wind: float32 [512, 4096], P(('lat', 'pole'), 'lon'), may hold values from -6 to 6
- depth: float32 [512, 4096], P('lat', 'lon'), may hold values from 0.5 to 2
- pole_real: float32 [16], P('pole'), may hold values from 0.5 to 2
- pole_imag: float32 [16], P('pole'), may hold values from -1.5 to 1.5
- weight_real: float32 [16], P('pole'), may hold values from -1 to 1
- weight_imag: float32 [16], P('pole'), may hold values from -1 to 1
Outputs:
- new_height: float32 [512, 4096], P(('lat', 'pole'), 'lon')
The draws below stay inside these ranges and needn't reach their ends.
All inputs are finite; a program needn't handle non-finite values.
Results may differ from the reference program's by a relative error of at most 0.000046.
Values sent between devices are 32-bit elements; how exact they have to be, the bound alone decides.
No kernel may reach another device: no remote copies, remote signals or barrier semaphores. Data moves between devices by JAX's collectives and lax.ppermute only.
A program may use at most 64 MiB of HBM per device.

```python
import math
import jax
import jax.numpy as jnp
from jax import lax

SWEEPS = 6
POLES = 16
NLAT = 512
NLON = 4096


def block_scale(rng, dims, split, smallest, high):
    level = 1.0
    for position, shards_of in split:
        steps = jax.random.uniform(jax.random.fold_in(jax.random.fold_in(rng, 6), position), (shards_of,), jnp.float32, smallest / len(split), high / len(split))
        level = level * jnp.repeat(jnp.exp(steps), dims[position] // shards_of).reshape((-1,) + (1,) * (len(dims) - 1 - position))
    return level


def scatter_about(own_key, extent, scale, reach, split=(), kind=jnp.bfloat16):
    array = jax.random.normal(own_key, extent, jnp.float32) * scale
    if len(split) > 0:
        array = block_scale(own_key, extent, split, -0.22, 0.18) * array
    return jnp.clip(array, min=-reach, max=reach).astype(kind)


def setup_inputs(seed: int = 0) -> dict:
    key_of = jax.random.split(jax.random.key(seed), 9)
    return {
        "height": scatter_about(key_of[0], (NLAT, NLON), 1.0, 6.0, ((0, 64), (1, 4)), jnp.float32),
        "east_wind": scatter_about(key_of[1], (NLAT, NLON), 1.0, 6.0, ((0, 64), (1, 4)), jnp.float32),
        "north_wind": scatter_about(key_of[2], (NLAT, NLON), 1.0, 6.0, ((0, 64), (1, 4)), jnp.float32),
        "depth": jnp.clip(jnp.exp(math.log(2.0) - 1.3862944 * jax.random.uniform(key_of[3], (NLAT, NLON), jnp.float32) ** block_scale(key_of[3], (NLAT, NLON), ((0, 4), (1, 4)), -0.2, 0.2)), 0.5, 2.0),
        "pole_real": jnp.clip(0.5 + 1.5 * jax.random.uniform(key_of[4], (POLES,), jnp.float32) ** block_scale(key_of[4], (POLES,), ((0, 16),), -0.2, 0.2), 0.5, 2.0),
        "pole_imag": jnp.clip(jax.random.uniform(key_of[5], (POLES,), jnp.float32, -1.5, 1.5) * block_scale(key_of[5], (POLES,), ((0, 16),), -0.4, 0.0), -1.5, 1.5),
        "weight_real": scatter_about(key_of[6], (POLES,), 0.25, 1.0, ((0, 16),), jnp.float32),
        "weight_imag": scatter_about(key_of[7], (POLES,), 0.25, 1.0, ((0, 16),), jnp.float32),
    }


coriolis_max = 1.0
zonal_coupling = 1.0
merid_coupling = 1.0
flux_scale = 0.5
north_scale = 0.25
relax_weights = (0.8, 1.0, 0.9, 1.0, 0.85, 1.0)


def row_terms(row_index, total_rows):
    theta = math.pi * ((row_index + 0.5) / total_rows - 0.5)
    cosine = jnp.cos(theta)
    coriolis = coriolis_max * jnp.sin(theta)
    coriolis_sq = coriolis * coriolis
    zonal_coef = zonal_coupling / (cosine * cosine + 0.01)
    east_coef = flux_scale / (cosine + 0.05)
    return coriolis_sq[:, None], zonal_coef[:, None], east_coef[:, None]


def sweep_from(padded, rhs, depth, zonal_coef, diag_real, diag_imag, inv_real, inv_imag, weight):
    centre = padded[:, 1:-1, 1:-1]
    zonal_sum = padded[:, 1:-1, 2:] + padded[:, 1:-1, :-2]
    merid_sum = padded[:, 2:, 1:-1] + padded[:, :-2, 1:-1]
    neigh = depth * (zonal_coef * zonal_sum + merid_coupling * merid_sum)
    phi_real = centre[0]
    phi_imag = centre[1]
    res_real = rhs + neigh[0] - (diag_real * phi_real - diag_imag * phi_imag)
    res_imag = neigh[1] - (diag_real * phi_imag + diag_imag * phi_real)
    new_real = phi_real + weight * (res_real * inv_real - res_imag * inv_imag)
    new_imag = phi_imag + weight * (res_real * inv_imag + res_imag * inv_real)
    return jnp.stack([new_real, new_imag])


def pad_field(stacked):
    beside_all = jnp.concatenate([stacked[:, :, -1:], stacked, stacked[:, :, :1]], axis=2)
    return jnp.pad(beside_all, ((0, 0), (1, 1), (0, 0)))


def reference(height, east_wind, north_wind, depth, pole_real, pole_imag, weight_real, weight_imag):
    total_rows = NLAT
    row_index = jnp.arange(total_rows).astype(jnp.float32)
    coriolis_sq, zonal_coef, east_coef = row_terms(row_index, total_rows)
    east_next = jnp.roll(east_wind, -1, axis=1)
    east_prev = jnp.roll(east_wind, 1, axis=1)
    partial_value = height - east_coef * (east_next - east_prev)
    north_pad = jnp.pad(north_wind, ((1, 1), (0, 0)))
    rhs = partial_value - north_scale * (north_pad[2:] - north_pad[:-2])
    diag_base = coriolis_sq + 2.0 * depth * (zonal_coef + merid_coupling)

    def one_pole(total, params):
        real_part, imag_part, wreal, wimag = params
        diag_real = real_part + diag_base
        denom = diag_real * diag_real + imag_part * imag_part
        inv_real = diag_real / denom
        inv_imag = -imag_part / denom
        phi = jnp.stack([rhs * inv_real, rhs * inv_imag])
        for step in range(SWEEPS):
            phi = sweep_from(pad_field(phi), rhs, depth, zonal_coef, diag_real, imag_part, inv_real, inv_imag, relax_weights[step])
        return total + (wreal * phi[0] - wimag * phi[1]), None

    start = jnp.zeros(height.shape, jnp.float32)
    total, unused = lax.scan(one_pole, start, (pole_real, pole_imag, weight_real, weight_imag))
    return total
```

```python
import math

import jax
import jax.numpy as jnp
from jax import lax
from jax.experimental import pallas as pl
from jax.experimental.pallas import tpu as pltpu
from jax.sharding import PartitionSpec as P

coriolis_max = 1.0
zonal_coupling = 1.0
merid_coupling = 1.0
flux_scale = 0.5
north_scale = 0.25
relax_weights = (0.8, 1.0, 0.9, 1.0, 0.85, 1.0)

POLES = 16
LANES = 128
ROWS = 8
COLS = 1024
HALO = 6
TILES = 9
WIDE = TILES * LANES
STEP = LANES - 2 * HALO
F32 = jnp.float32

VMEM = pl.BlockSpec(memory_space=pltpu.VMEM)


def row_terms(row_index, total_rows):
    theta = math.pi * ((row_index + 0.5) / total_rows - 0.5)
    cosine = jnp.cos(theta)
    coriolis = coriolis_max * jnp.sin(theta)
    coriolis_sq = coriolis * coriolis
    zonal_coef = zonal_coupling / (cosine * cosine + 0.01)
    east_coef = flux_scale / (cosine + 0.05)
    return coriolis_sq, zonal_coef, east_coef


def near_depth(depth_ref, block, columns):
    last = depth_ref.shape[0] // ROWS - 1
    rows = [jnp.maximum(block - 1, 0), block, jnp.minimum(block + 1, last)]
    return [depth_ref[pl.ds(pl.multiple_of(r * ROWS, ROWS), ROWS), columns] for r in rows]


def edges_kernel(height, east, north, depth, to_right, to_left):
    block = lax.axis_index("pole")
    for out, first in ((to_right, COLS - LANES), (to_left, 0)):
        columns = slice(first, first + LANES)
        parts = [height[:, columns], east[:, columns], north[:, columns]]
        parts += near_depth(depth, block, columns)
        for i, part in enumerate(parts):
            out[i * ROWS : (i + 1) * ROWS, :] = part


def rows_kernel(height, east, north, depth, from_left, from_right, east_coef, field, winds, depths, send_near, send_far):
    block = lax.axis_index("pole")
    even = lax.rem(block, 2) == 0
    lane = lax.broadcasted_iota(jnp.int32, (ROWS, LANES), 1)
    row = lax.broadcasted_iota(jnp.int32, (ROWS, WIDE), 0)

    def widened(own, part):
        at = slice(part * ROWS, (part + 1) * ROWS)
        return jnp.concatenate([own, jnp.where(lane < LANES // 2, from_right[at, :], from_left[at, :])], axis=1)

    high = widened(height[...], 0)
    eastward = widened(east[...], 1)
    northward = widened(north[...], 2)
    coef = jnp.concatenate([east_coef[...]] * TILES, axis=1)
    partial = high - coef * (pltpu.roll(eastward, WIDE - 1, 1) - pltpu.roll(eastward, 1, 1))
    below = jnp.where(row == ROWS - 1, 0.0, pltpu.roll(northward, ROWS - 1, 0))
    above = jnp.where(row == 0, 0.0, pltpu.roll(northward, 1, 0))
    partial = partial - north_scale * (below - above)
    field[...] = partial
    winds[...] = northward
    upward = jnp.where(row < HALO, partial, pltpu.roll(northward, HALO, 0))
    downward = jnp.where(row < HALO, pltpu.roll(partial, ROWS - 2, 0), pltpu.roll(northward, ROWS - 1, 0))
    send_near[...] = jnp.where(even, downward, upward)
    send_far[0:ROWS, :] = jnp.where(even, upward, downward)
    for i, part in enumerate(near_depth(depth, block, slice(None))):
        part = widened(part, 3 + i)
        depths[i * ROWS : (i + 1) * ROWS, :] = part
        if i == 1:
            send_far[ROWS : 2 * ROWS, :] = part


def solve_kernel(field, winds, depths, near, far, table, coriolis, zonal, out, rhs_w, depth_w, base_w, zonal_w, gain, total, result):
    block = lax.axis_index("pole")
    band = lax.axis_index("lat")
    even = lax.rem(block, 2) == 0
    top = jnp.logical_and(band == 0, block == 0)
    last_block = lax.axis_size("pole") - 1
    bottom = jnp.logical_and(band == lax.axis_size("lat") - 1, block == last_block)
    row = lax.broadcasted_iota(jnp.int32, (ROWS, WIDE), 0)

    near_rows, far_rows, far_depth = near[...], far[0:ROWS, :], far[ROWS : 2 * ROWS, :]
    upper = jnp.where(top, 0.0, jnp.where(even, far_rows, near_rows))
    lower = jnp.where(bottom, 0.0, jnp.where(even, near_rows, far_rows))
    north = winds[...]
    from_above = north_scale * pltpu.roll(upper, ROWS - HALO, 0)
    from_below = north_scale * pltpu.roll(lower, 1, 0)
    mid = field[...] + jnp.where(row == 0, from_above, 0.0) - jnp.where(row == ROWS - 1, from_below, 0.0)
    own_first = jnp.where(top, 0.0, north_scale * pltpu.roll(north, ROWS - 1, 0))
    own_last = jnp.where(bottom, 0.0, north_scale * pltpu.roll(north, 1, 0))
    above = pltpu.roll(upper, ROWS - HALO, 0) - jnp.where(row == ROWS - 1, own_first, 0.0)
    below = lower + jnp.where(row == 0, own_last, 0.0)
    d_above = jnp.where(block == 0, far_depth, depths[0:ROWS, :])
    d_mid = depths[ROWS : 2 * ROWS, :]
    d_below = jnp.where(block == last_block, far_depth, depths[2 * ROWS : 3 * ROWS, :])

    def window(wide, t):
        first = t * STEP - HALO
        tile, shift = divmod(first, LANES)
        if tile < 0:
            pair = jnp.concatenate([wide[:, WIDE - LANES :], wide[:, :LANES]], axis=1)
        else:
            pair = wide[:, tile * LANES : (tile + 2) * LANES]
        return pltpu.roll(pair, 2 * LANES - shift, 1)[:, :LANES]

    for i, (rhs, deep) in enumerate(((above, d_above), (mid, d_mid), (below, d_below))):
        at = slice(i * ROWS, (i + 1) * ROWS)
        z = zonal[at, :]
        for t in range(TILES):
            d = window(deep, t)
            rhs_w[t, at, :] = window(rhs, t) / d
            depth_w[t, at, :] = d
            base_w[t, at, :] = coriolis[at, :] + 2.0 * d * (z + merid_coupling)
        zonal_w[at, :] = z

    sub = lax.broadcasted_iota(jnp.int32, (ROWS, LANES), 0)
    lane = lax.broadcasted_iota(jnp.int32, (ROWS, LANES), 1)
    numbers = jnp.broadcast_to(table[...] + near[ROWS - 1 : ROWS, 0:LANES], (ROWS, LANES))

    def number(which, group):
        picked = jnp.where(lane == which * POLES + group * ROWS + sub, numbers, 0.0)
        return jnp.broadcast_to(jnp.sum(picked, axis=1, keepdims=True), (ROWS, LANES))

    groups = POLES // ROWS
    params = [[number(which, g) for which in range(4)] for g in range(groups)]
    first, end = ROWS - HALO, 2 * ROWS + HALO

    def one_window(t, carry):
        sums = [jnp.zeros((ROWS, LANES), F32)] * ROWS
        for g in range(groups):
            real, imag, wreal, wimag = params[g]
            imag_sq = imag * imag
            p_real, p_imag = {}, {}
            for j in range(first, end):
                d = jnp.broadcast_to(depth_w[t, j : j + 1, :], (ROWS, LANES))
                if j < ROWS:
                    d = jnp.where(top, 0.0, d)
                if j >= 2 * ROWS:
                    d = jnp.where(bottom, 0.0, d)
                diag = real + jnp.broadcast_to(base_w[t, j : j + 1, :], (ROWS, LANES))
                scale = d / (diag * diag + imag_sq)
                g_real = scale * diag
                g_imag = -(scale * imag)
                gain[0, j] = g_real
                gain[1, j] = g_imag
                r = jnp.broadcast_to(rhs_w[t, j : j + 1, :], (ROWS, LANES))
                p_real[j] = r * g_real
                p_imag[j] = r * g_imag
            alpha = 1.0
            for m, w in enumerate(relax_weights):
                n_real, n_imag = {}, {}
                for j in range(first + m + 1, end - m - 1):
                    z = jnp.broadcast_to(zonal_w[j : j + 1, :], (ROWS, LANES))
                    r = jnp.broadcast_to(rhs_w[t, j : j + 1, :], (ROWS, LANES))
                    if alpha != 1.0:
                        r = r * (1.0 / alpha)
                    s_real = z * (pltpu.roll(p_real[j], 1, 1) + pltpu.roll(p_real[j], LANES - 1, 1))
                    s_real = r + s_real + (p_real[j - 1] + p_real[j + 1])
                    s_imag = z * (pltpu.roll(p_imag[j], 1, 1) + pltpu.roll(p_imag[j], LANES - 1, 1))
                    s_imag = s_imag + (p_imag[j - 1] + p_imag[j + 1])
                    g_real, g_imag = gain[0, j], gain[1, j]
                    u_real = s_real * g_real - s_imag * g_imag
                    u_imag = s_real * g_imag + s_imag * g_real
                    if w != 1.0:
                        u_real = u_real + ((1.0 - w) / w) * p_real[j]
                        u_imag = u_imag + ((1.0 - w) / w) * p_imag[j]
                    n_real[j], n_imag[j] = u_real, u_imag
                p_real, p_imag = n_real, n_imag
                alpha = alpha * w
            wreal, wimag = alpha * wreal, alpha * wimag
            for j in range(ROWS):
                sums[j] = sums[j] + (wreal * p_real[ROWS + j] - wimag * p_imag[ROWS + j])
        for j in range(ROWS):
            result[t, j : j + 1, :] = jnp.sum(sums[j], axis=0, keepdims=True)
        return carry

    lax.fori_loop(0, TILES, one_window, 0)

    for q in range(COLS // LANES):
        value = jnp.zeros((ROWS, LANES), F32)
        for t in range(TILES):
            begin, stop = max(t * STEP, q * LANES), min((t + 1) * STEP, (q + 1) * LANES)
            if begin < stop:
                shift = (t * STEP - HALO - q * LANES) % LANES
                moved = pltpu.roll(result[t], shift, 1) if shift else result[t]
                inside = jnp.logical_and(lane >= begin - q * LANES, lane < stop - q * LANES)
                value = jnp.where(inside, moved, value)
        out[:, q * LANES : (q + 1) * LANES] = value


def shape(*dims):
    return jax.ShapeDtypeStruct(dims, F32)


def call(kernel, outs, n_in, flops, scratch=()):
    return pl.pallas_call(
        kernel,
        out_shape=outs,
        in_specs=[VMEM] * n_in,
        out_specs=[VMEM] * len(outs),
        scratch_shapes=list(scratch),
        cost_estimate=pl.CostEstimate(flops=flops, bytes_accessed=200000, transcendentals=0),
        compiler_params=pltpu.CompilerParams(vmem_limit_bytes=32 * 1024 * 1024),
    )


def body(height, east_wind, north_wind, depth, pole_real, pole_imag, weight_real, weight_imag):
    n_pole, n_lat, n_lon = (lax.axis_size(a) for a in ("pole", "lat", "lon"))
    pole, lat = lax.axis_index("pole"), lax.axis_index("lat")
    total_rows = depth.shape[0] * n_lat
    first_row = (lat * n_pole + pole) * ROWS - ROWS
    rows = (first_row + lax.broadcasted_iota(jnp.int32, (3 * ROWS, LANES), 0)).astype(F32)
    coriolis, zonal, east_coef = row_terms(rows, total_rows)

    at = lax.broadcasted_iota(jnp.int32, (1, LANES), 1)
    table = jnp.zeros((1, LANES), F32)
    for i, value in enumerate((pole_real, pole_imag, weight_real, weight_imag)):
        table = jnp.where(at == i * POLES + pole, value[0], table)
    layers = n_pole // 2
    for partner in (lambda z: layers - 1 - z, lambda z: z ^ 2, lambda z: z ^ 1):
        pairs = [(2 * z + x, 2 * partner(z) + x) for z in range(layers) for x in range(2)]
        table = table + lax.ppermute(table, "pole", pairs)

    to_right, to_left = call(edges_kernel, [shape(6 * ROWS, LANES)] * 2, 4, 10000)(height, east_wind, north_wind, depth)
    from_left = lax.ppermute(to_right, "lon", [(i, (i + 1) % n_lon) for i in range(n_lon)])
    from_right = lax.ppermute(to_left, "lon", [((i + 1) % n_lon, i) for i in range(n_lon)])
    wide, both = shape(ROWS, WIDE), shape(2 * ROWS, WIDE)
    field, winds, depths, send_near, send_far = call(
        rows_kernel, [wide, wide, shape(3 * ROWS, WIDE), wide, both], 7, 100000
    )(height, east_wind, north_wind, depth, from_left, from_right, east_coef[ROWS : 2 * ROWS])

    total = n_lat * n_pole
    far_pairs = []
    for r in range(1, total, 2):
        for c in range(n_lon):
            one, two = (((b % n_pole) * n_lat + b // n_pole) * n_lon + c for b in (r, (r + 1) % total))
            far_pairs += [(one, two), (two, one)]
    far = lax.ppermute(send_far, ("pole", "lat", "lon"), far_pairs)
    send_near = lax.dynamic_update_slice(send_near, table, (ROWS - 1, 0))
    near = lax.ppermute(send_near, "pole", [(i, i ^ 1) for i in range(n_pole)])

    scratch = [
        pltpu.VMEM((TILES, 3 * ROWS, LANES), F32),
        pltpu.VMEM((TILES, 3 * ROWS, LANES), F32),
        pltpu.VMEM((TILES, 3 * ROWS, LANES), F32),
        pltpu.VMEM((3 * ROWS, LANES), F32),
        pltpu.VMEM((2, 3 * ROWS, ROWS, LANES), F32),
        pltpu.VMEM((ROWS, LANES), F32),
        pltpu.VMEM((TILES, ROWS, LANES), F32),
    ]
    (out,) = call(solve_kernel, [shape(ROWS, COLS)], 8, 60000000, scratch)(
        field, winds, depths, near, far, table, coriolis, zonal
    )
    return out


def solution(mesh):
    rows = P(("lat", "pole"), "lon")
    one = P("pole")
    in_specs = (rows, rows, rows, P("lat", "lon"), one, one, one, one)
    return jax.shard_map(body, mesh=mesh, in_specs=in_specs, out_specs=rows, check_vma=False)
```

```python
import math

import jax
import jax.numpy as jnp
from jax import lax
from jax.experimental import pallas as pl
from jax.experimental.pallas import tpu as pltpu
from jax.sharding import PartitionSpec as P

coriolis_max = 1.0
zonal_coupling = 1.0
merid_coupling = 1.0
flux_scale = 0.5
north_scale = 0.25
relax_weights = (0.8, 1.0, 0.9, 1.0, 0.85, 1.0)

POLES = 16
LANES = 128
ROWS = 8
COLS = 1024
HALO = 6
TILES = 9
WIDE = TILES * LANES
INVERSE = pow(TILES, -1, LANES)
F32 = jnp.float32
LIMIT = 24 * 1024 * 1024

VMEM = pl.BlockSpec(memory_space=pltpu.VMEM)


def row_terms(row_index, total_rows):
    theta = math.pi * ((row_index + 0.5) / total_rows - 0.5)
    cosine = jnp.cos(theta)
    coriolis = coriolis_max * jnp.sin(theta)
    coriolis_sq = coriolis * coriolis
    zonal_coef = zonal_coupling / (cosine * cosine + 0.01)
    east_coef = flux_scale / (cosine + 0.05)
    return coriolis_sq, zonal_coef, east_coef


def near_depth(depth_at, block, depth_rows, columns):
    last = depth_rows // ROWS - 1
    rows = [jnp.maximum(block - 1, 0), block, jnp.minimum(block + 1, last)]
    return [depth_at[pl.ds(pl.multiple_of(r * ROWS, ROWS), ROWS), columns] for r in rows]


def edges_kernel(height, east, north, depth, to_right, to_left, around, sems):
    block = lax.axis_index("pole")
    copies = []
    for out, first in ((to_right, COLS - LANES), (to_left, 0)):
        columns = pl.ds(first, LANES)
        parts = [height.at[:, columns], east.at[:, columns], north.at[:, columns]]
        parts += near_depth(depth.at, block, depth.shape[0], columns)
        copies += [(part, out.at[pl.ds(i * ROWS, ROWS), :]) for i, part in enumerate(parts)]
    parts = near_depth(depth.at, block, depth.shape[0], pl.ds(0, COLS))
    copies += [(part, around.at[pl.ds(i * ROWS, ROWS), :]) for i, part in enumerate(parts)]
    copies = [pltpu.make_async_copy(source, target, sems.at[i]) for i, (source, target) in enumerate(copies)]
    for copy in copies:
        copy.start()
    for copy in copies:
        copy.wait()


def near_kernel(rows, one, two, after, out):
    out[0 : ROWS - 1, :] = rows[0 : ROWS - 1, :]
    out[ROWS - 1 : ROWS, 0:LANES] = one[...] + two[...]
    out[ROWS - 1 : ROWS, LANES:] = rows[ROWS - 1 : ROWS, LANES:]


def rows_kernel(height, east, north, around, from_left, from_right, after, field, winds, depths, send_near, send_far, coriolis, zonal):
    block, band = lax.axis_index("pole"), lax.axis_index("lat")
    total_rows = lax.axis_size("lat") * lax.axis_size("pole") * ROWS
    first_row = (band * lax.axis_size("pole") + block) * ROWS - ROWS
    index = (first_row + lax.broadcasted_iota(jnp.int32, (3 * ROWS, LANES), 0)).astype(F32)
    coriolis[...], zonal[...], east_coef = row_terms(index, total_rows)
    east_coef = east_coef[ROWS : 2 * ROWS, :]
    even = lax.rem(block, 2) == 0
    lane = lax.broadcasted_iota(jnp.int32, (ROWS, LANES), 1)
    row = lax.broadcasted_iota(jnp.int32, (ROWS, WIDE), 0)

    def widened(own, part):
        at = slice(part * ROWS, (part + 1) * ROWS)
        return jnp.concatenate([own, jnp.where(lane < LANES // 2, from_right[at, :], from_left[at, :])], axis=1)

    high = widened(height[...], 0)
    eastward = widened(east[...], 1)
    northward = widened(north[...], 2)
    coef = jnp.concatenate([east_coef] * TILES, axis=1)
    partial = high - coef * (pltpu.roll(eastward, WIDE - 1, 1) - pltpu.roll(eastward, 1, 1))
    below = jnp.where(row == ROWS - 1, 0.0, pltpu.roll(northward, ROWS - 1, 0))
    above = jnp.where(row == 0, 0.0, pltpu.roll(northward, 1, 0))
    partial = partial - north_scale * (below - above)
    field[...] = partial
    winds[...] = northward
    upward = jnp.where(row < HALO, partial, pltpu.roll(northward, HALO, 0))
    downward = jnp.where(row < HALO, pltpu.roll(partial, ROWS - 2, 0), pltpu.roll(northward, ROWS - 1, 0))
    send_near[...] = jnp.where(even, downward, upward)
    send_far[0:ROWS, :] = jnp.where(even, upward, downward)
    for i in range(3):
        part = widened(around[i * ROWS : (i + 1) * ROWS, :], 3 + i)
        depths[i * ROWS : (i + 1) * ROWS, :] = part
        if i == 1:
            send_far[ROWS : 2 * ROWS, :] = part


def solve_kernel(field, winds, depths, near, far, one, two, coriolis, zonal, out, rhs_w, depth_w, base_w, poles, gain, even_p, odd_p, result):
    block = lax.axis_index("pole")
    band = lax.axis_index("lat")
    even = lax.rem(block, 2) == 0
    top = jnp.logical_and(band == 0, block == 0)
    last_block = lax.axis_size("pole") - 1
    bottom = jnp.logical_and(band == lax.axis_size("lat") - 1, block == last_block)
    row = lax.broadcasted_iota(jnp.int32, (ROWS, WIDE), 0)

    near_rows, far_rows, far_depth = near[...], far[0:ROWS, :], far[ROWS : 2 * ROWS, :]
    upper = jnp.where(top, 0.0, jnp.where(even, far_rows, near_rows))
    lower = jnp.where(bottom, 0.0, jnp.where(even, near_rows, far_rows))
    north = winds[...]
    from_above = north_scale * pltpu.roll(upper, ROWS - HALO, 0)
    from_below = north_scale * pltpu.roll(lower, 1, 0)
    mid = field[...] + jnp.where(row == 0, from_above, 0.0) - jnp.where(row == ROWS - 1, from_below, 0.0)
    own_first = jnp.where(top, 0.0, north_scale * pltpu.roll(north, ROWS - 1, 0))
    own_last = jnp.where(bottom, 0.0, north_scale * pltpu.roll(north, 1, 0))
    above = pltpu.roll(upper, ROWS - HALO, 0) - jnp.where(row == ROWS - 1, own_first, 0.0)
    below = lower + jnp.where(row == 0, own_last, 0.0)
    d_above = jnp.where(block == 0, far_depth, depths[0:ROWS, :])
    d_mid = depths[ROWS : 2 * ROWS, :]
    d_below = jnp.where(block == last_block, far_depth, depths[2 * ROWS : 3 * ROWS, :])

    lane = lax.broadcasted_iota(jnp.int32, (ROWS, LANES), 1)
    sub = lax.broadcasted_iota(jnp.int32, (ROWS, LANES), 0)

    def owner(tile):
        return lax.rem(tile * LANES + lane, TILES)

    def dealt(wide, t):
        value = wide[:, 0:LANES]
        for q in range(1, TILES):
            value = jnp.where(owner(q) == t, wide[:, q * LANES : (q + 1) * LANES], value)
        return jnp.take_along_axis(value, lax.rem(lane * TILES + t, LANES), axis=1)

    for i, (rhs, deep) in enumerate(((above, d_above), (mid, d_mid), (below, d_below))):
        at = slice(i * ROWS, (i + 1) * ROWS)
        z = zonal[at, :]
        for t in range(TILES):
            d = dealt(deep, t)
            rhs_w[t, at, :] = dealt(rhs, t) / d
            base_w[t, at, :] = coriolis[at, :] + 2.0 * d * (z + merid_coupling)
            if i == 0:
                d = jnp.where(top, 0.0, d)
            if i == 2:
                d = jnp.where(bottom, 0.0, d)
            depth_w[t, at, :] = d

    numbers = jnp.broadcast_to((one[...] + two[...]) + near[ROWS - 1 : ROWS, 0:LANES], (ROWS, LANES))
    groups = POLES // ROWS
    for g in range(groups):
        for which in range(4):
            picked = jnp.where(lane == which * POLES + g * ROWS + sub, numbers, 0.0)
            poles[g, which] = jnp.broadcast_to(jnp.sum(picked, axis=1, keepdims=True), (ROWS, LANES))
    first, end = ROWS - HALO, 2 * ROWS + HALO

    def spread(ref, j, *index):
        return jnp.broadcast_to(ref[(*index, slice(j, j + 1), slice(None))], (ROWS, LANES))

    def begin(i, carry):
        g, t = i // TILES, lax.rem(i, TILES)
        real, imag = poles[g, 0], poles[g, 1]
        imag_sq = imag * imag
        for j in range(first, end):
            diag = real + spread(base_w, j, t)
            scale = spread(depth_w, j, t) / (diag * diag + imag_sq)
            g_real, g_imag = scale * diag, -(scale * imag)
            gain[g, 0, j, t] = g_real
            gain[g, 1, j, t] = g_imag
            r = spread(rhs_w, j, t)
            even_p[g, 0, j, t] = r * g_real
            even_p[g, 1, j, t] = r * g_imag
        return carry

    lax.fori_loop(0, groups * TILES, begin, 0)
    alpha = 1.0
    for m, w in enumerate(relax_weights):
        old, new = (even_p, odd_p) if m % 2 == 0 else (odd_p, even_p)
        low, high = first + m + 1, end - m - 1
        last = m == len(relax_weights) - 1

        def one_row(g, j):
            z = jnp.broadcast_to(zonal[pl.ds(j, 1), :], (ROWS, LANES))
            here = [[old[g, c, j, t] for t in range(TILES)] for c in range(2)]
            west = [pltpu.roll(here[c][TILES - 1], 1, 1) for c in range(2)]
            east = [pltpu.roll(here[c][0], LANES - 1, 1) for c in range(2)]
            for t in range(TILES):
                s_real, s_imag = (
                    z * ((here[c][t - 1] if t else west[c]) + (here[c][t + 1] if t < TILES - 1 else east[c]))
                    + (old[g, c, j - 1, t] + old[g, c, j + 1, t])
                    for c in range(2)
                )
                s_real = s_real + jnp.broadcast_to(rhs_w[t, pl.ds(j, 1), :], (ROWS, LANES))
                g_real, g_imag = gain[g, 0, j, t], gain[g, 1, j, t]
                u_real = s_real * g_real - s_imag * g_imag
                u_imag = s_real * g_imag + s_imag * g_real
                if w != 1.0:
                    u_real = u_real + ((1.0 - w) / w) * here[0][t]
                    u_imag = u_imag + ((1.0 - w) / w) * here[1][t]
                if last:
                    wreal, wimag = alpha * poles[g, 2], alpha * poles[g, 3]
                    value = jnp.sum(wreal * u_real - wimag * u_imag, axis=0, keepdims=True)
                    result[g, t, pl.ds(j - ROWS, 1), :] = value
                else:
                    new[g, 0, j, t] = u_real
                    new[g, 1, j, t] = u_imag

        def sweep(i, carry):
            for g in range(groups):
                for k in range(2):
                    one_row(g, low + 2 * i + k)
            return carry

        lax.fori_loop(0, (high - low) // 2, sweep, 0)
        if w != 1.0:
            alpha = alpha * w
            rhs_w[...] = rhs_w[...] * (1.0 / w)

    undealt = []
    for t in range(TILES):
        value = result[0, t]
        for g in range(1, groups):
            value = value + result[g, t]
        index = lax.rem((lane - t + LANES) * INVERSE, LANES)
        undealt.append(jnp.take_along_axis(value, index, axis=1))
    for q in range(COLS // LANES):
        value = undealt[0]
        for t in range(1, TILES):
            value = jnp.where(owner(q) == t, undealt[t], value)
        out[:, q * LANES : (q + 1) * LANES] = value


def shape(*dims):
    return jax.ShapeDtypeStruct(dims, F32)


def call(kernel, outs, n_in, flops, scratch=()):
    return pl.pallas_call(
        kernel,
        out_shape=outs,
        in_specs=[VMEM] * n_in,
        out_specs=[VMEM] * len(outs),
        scratch_shapes=list(scratch),
        cost_estimate=pl.CostEstimate(flops=flops, bytes_accessed=200000, transcendentals=0),
        compiler_params=pltpu.CompilerParams(vmem_limit_bytes=LIMIT),
    )


def body(height, east_wind, north_wind, depth, pole_real, pole_imag, weight_real, weight_imag):
    n_pole, n_lat, n_lon = (lax.axis_size(a) for a in ("pole", "lat", "lon"))
    pole = lax.axis_index("pole")
    at = lax.broadcasted_iota(jnp.int32, (1, LANES), 1)
    table = jnp.zeros((1, LANES), F32)
    for i, value in enumerate((pole_real, pole_imag, weight_real, weight_imag)):
        table = jnp.where(at == i * POLES + pole, value[0], table)
    layers = n_pole // 2

    def swapped(table, partner):
        pairs = [(2 * z + x, 2 * partner(z) + x) for z in range(layers) for x in range(2)]
        return lax.ppermute(table, "pole", pairs)

    table = first = (table + swapped(table, lambda z: layers - 1 - z))[0:1]
    table = table + swapped(table, lambda z: z ^ 2)
    third = swapped(table, lambda z: z ^ 1)

    column = shape(6 * ROWS, LANES)
    to_right, to_left, around = pl.pallas_call(
        edges_kernel,
        out_shape=[column, column, shape(3 * ROWS, COLS)],
        in_specs=[pl.BlockSpec(memory_space=pl.ANY)] * 4,
        out_specs=[VMEM] * 3,
        scratch_shapes=[pltpu.SemaphoreType.DMA((15,))],
        compiler_params=pltpu.CompilerParams(vmem_limit_bytes=66600000),
    )(height, east_wind, north_wind, depth)
    from_left = lax.ppermute(to_right, "lon", [(i, (i + 1) % n_lon) for i in range(n_lon)])
    from_right = lax.ppermute(to_left, "lon", [((i + 1) % n_lon, i) for i in range(n_lon)])
    wide, both = shape(ROWS, WIDE), shape(2 * ROWS, WIDE)
    terms = shape(3 * ROWS, LANES)
    field, winds, depths, send_near, send_far, coriolis, zonal = call(
        rows_kernel, [wide, wide, shape(3 * ROWS, WIDE), wide, both, terms, terms], 7, 100000
    )(height, east_wind, north_wind, around, from_left, from_right, first)

    total = n_lat * n_pole
    far_pairs = []
    for r in range(1, total, 2):
        for c in range(n_lon):
            one, two = (((b % n_pole) * n_lat + b // n_pole) * n_lon + c for b in (r, (r + 1) % total))
            far_pairs += [(one, two), (two, one)]
    far = lax.ppermute(send_far, ("pole", "lat", "lon"), far_pairs)
    (send_near,) = pl.pallas_call(
        near_kernel,
        out_shape=[wide],
        in_specs=[VMEM, VMEM, VMEM, pl.BlockSpec(memory_space=pl.ANY)],
        out_specs=[VMEM],
        compiler_params=pltpu.CompilerParams(vmem_limit_bytes=LIMIT),
    )(send_near, table, third, first)
    near = lax.ppermute(send_near, "pole", [(i, i ^ 1) for i in range(n_pole)])

    groups = POLES // ROWS
    tiles = pltpu.VMEM((TILES, 3 * ROWS, LANES), F32)
    iterate = pltpu.VMEM((groups, 2, 3 * ROWS, TILES, ROWS, LANES), F32)
    scratch = [
        tiles,
        tiles,
        tiles,
        pltpu.VMEM((groups, 4, ROWS, LANES), F32),
        pltpu.VMEM((groups, 2, 3 * ROWS, TILES, ROWS, LANES), F32),
        iterate,
        iterate,
        pltpu.VMEM((groups, TILES, ROWS, LANES), F32),
    ]
    (out,) = call(solve_kernel, [shape(ROWS, COLS)], 9, 60000000, scratch)(
        field, winds, depths, near, far, table, third, coriolis, zonal
    )
    return out


def solution(mesh):
    rows = P(("lat", "pole"), "lon")
    one = P("pole")
    in_specs = (rows, rows, rows, P("lat", "lon"), one, one, one, one)
    return jax.shard_map(body, mesh=mesh, in_specs=in_specs, out_specs=rows, check_vma=False)
```

```python
import math

import jax
import jax.numpy as jnp
from jax import lax
from jax.experimental import pallas as pl
from jax.experimental.pallas import tpu as pltpu
from jax.sharding import PartitionSpec as P

coriolis_max = 1.0
zonal_coupling = 1.0
merid_coupling = 1.0
flux_scale = 0.5
north_scale = 0.25
relax_weights = (0.8, 1.0, 0.9, 1.0, 0.85, 1.0)

POLES = 16
LANES = 128
ROWS = 8
COLS = 1024
HALO = 6
TILES = 9
WIDE = TILES * LANES
INVERSE = pow(TILES, -1, LANES)
F32 = jnp.float32
LIMIT = 24 * 1024 * 1024

VMEM = pl.BlockSpec(memory_space=pltpu.VMEM)


def row_terms(row_index, total_rows):
    theta = math.pi * ((row_index + 0.5) / total_rows - 0.5)
    cosine = jnp.cos(theta)
    coriolis = coriolis_max * jnp.sin(theta)
    coriolis_sq = coriolis * coriolis
    zonal_coef = zonal_coupling / (cosine * cosine + 0.01)
    east_coef = flux_scale / (cosine + 0.05)
    return coriolis_sq, zonal_coef, east_coef


def at_top():
    return jnp.logical_and(lax.axis_index("lat") == 0, lax.axis_index("pole") == 0)


def at_bottom():
    last_band = lax.axis_index("lat") == lax.axis_size("lat") - 1
    return jnp.logical_and(last_band, lax.axis_index("pole") == lax.axis_size("pole") - 1)


def terms_near(blocks):
    n_pole = lax.axis_size("pole")
    first = (lax.axis_index("lat") * n_pole + lax.axis_index("pole") - blocks) * ROWS
    index = first + lax.broadcasted_iota(jnp.int32, ((2 * blocks + 1) * ROWS, LANES), 0)
    return row_terms(index.astype(F32), lax.axis_size("lat") * n_pole * ROWS)


def own_field(high, eastward, northward, coef):
    column = lax.broadcasted_iota(jnp.int32, (ROWS, COLS), 1)
    row = lax.broadcasted_iota(jnp.int32, (ROWS, COLS), 0)
    lane = lax.broadcasted_iota(jnp.int32, (ROWS, LANES), 1)
    coef = jnp.concatenate([coef] * (COLS // LANES), axis=1)
    after = jnp.where(column == COLS - 1, 0.0, pltpu.roll(eastward, COLS - 1, 1))
    before = jnp.where(column == 0, 0.0, pltpu.roll(eastward, 1, 1))
    below = jnp.where(row == ROWS - 1, 0.0, pltpu.roll(northward, ROWS - 1, 0))
    above = jnp.where(row == 0, 0.0, pltpu.roll(northward, 1, 0))
    partial = high - coef * (after - before) - north_scale * (below - above)
    outer = jnp.where(lane < LANES // 2, eastward[:, 0:LANES], eastward[:, COLS - LANES :])
    nothing = jnp.zeros((ROWS, LANES), F32)
    return jnp.concatenate([partial, outer], axis=1), jnp.concatenate([northward, nothing], axis=1)


def rows_kernel(height, east, north, depth, send_near, send_far, fields, sems):
    block = lax.axis_index("pole")
    own = pl.ds(pl.multiple_of(block * ROWS, ROWS), ROWS)
    copies = [pltpu.make_async_copy(source, fields.at[i], sems.at[i]) for i, source in enumerate((height, east, north))]
    copies.append(pltpu.make_async_copy(depth.at[own, :], fields.at[3], sems.at[3]))
    for copy in copies:
        copy.start()
    unused, also_unused, coef = terms_near(0)
    for copy in copies:
        copy.wait()
    even = lax.rem(block, 2) == 0
    row = lax.broadcasted_iota(jnp.int32, (ROWS, WIDE), 0)
    partial, northward = own_field(fields[0], fields[1], fields[2], coef)
    upward = jnp.where(row < HALO, partial, pltpu.roll(northward, HALO, 0))
    downward = jnp.where(row < HALO, pltpu.roll(partial, ROWS - 2, 0), pltpu.roll(northward, ROWS - 1, 0))
    send_near[...] = jnp.where(even, downward, upward)
    send_far[0:ROWS, :] = jnp.where(even, upward, downward)
    send_far[ROWS : 2 * ROWS, 0:COLS] = fields[3]
    send_far[ROWS : 2 * ROWS, COLS:] = jnp.zeros((ROWS, LANES), F32)


def columns_kernel(height, east, north, depth, near, far, field, depths, coriolis, zonal, east_coef, to_right, to_left):
    block = lax.axis_index("pole")
    even = lax.rem(block, 2) == 0
    top, bottom, last_block = at_top(), at_bottom(), lax.axis_size("pole") - 1
    coriolis[...], zonal[...], coef = terms_near(1)
    east_coef[...] = coef
    row = lax.broadcasted_iota(jnp.int32, (ROWS, WIDE), 0)
    lane = lax.broadcasted_iota(jnp.int32, (ROWS, LANES), 1)
    partial, northward = own_field(height[...], east[...], north[...], coef[ROWS : 2 * ROWS, :])

    near_rows, far_rows, far_depth = near[...], far[0:ROWS, :], far[ROWS : 2 * ROWS, 0:COLS]
    upper = jnp.where(top, 0.0, jnp.where(even, far_rows, near_rows))
    lower = jnp.where(bottom, 0.0, jnp.where(even, near_rows, far_rows))
    from_above = north_scale * pltpu.roll(upper, ROWS - HALO, 0)
    from_below = north_scale * pltpu.roll(lower, 1, 0)
    mid = partial + jnp.where(row == 0, from_above, 0.0) - jnp.where(row == ROWS - 1, from_below, 0.0)
    own_first = jnp.where(top, 0.0, north_scale * pltpu.roll(northward, ROWS - 1, 0))
    own_last = jnp.where(bottom, 0.0, north_scale * pltpu.roll(northward, 1, 0))
    above = pltpu.roll(upper, ROWS - HALO, 0) - jnp.where(row == ROWS - 1, own_first, 0.0)
    below = lower + jnp.where(row == 0, own_last, 0.0)
    rows = [jnp.maximum(block - 1, 0), block, jnp.minimum(block + 1, last_block)]
    deep = [depth[pl.ds(pl.multiple_of(r * ROWS, ROWS), ROWS), :] for r in rows]
    deep[0] = jnp.where(block == 0, far_depth, deep[0])
    deep[2] = jnp.where(block == last_block, far_depth, deep[2])
    for i, (value, d) in enumerate(zip((above, mid, below), deep)):
        at, later = slice(i * ROWS, (i + 1) * ROWS), slice((3 + i) * ROWS, (4 + i) * ROWS)
        field[at, :] = value
        depths[at, :] = d
        winds = value[:, COLS:]
        to_right[at, :] = jnp.where(lane == 0, pltpu.roll(winds, 1, 1), value[:, COLS - LANES : COLS])
        to_left[at, :] = jnp.where(lane == LANES - 1, pltpu.roll(winds, LANES - 1, 1), value[:, 0:LANES])
        to_right[later, :] = d[:, COLS - LANES :]
        to_left[later, :] = d[:, 0:LANES]


def merge_kernel(one, two, after, out):
    out[...] = one[...] + two[...]


def solve_kernel(field, depths, from_left, from_right, one, two, coriolis, zonal, east, out, rhs_w, depth_w, base_w, poles, gain, even_p, odd_p, result):
    top, bottom = at_top(), at_bottom()
    tile_lane = lax.broadcasted_iota(jnp.int32, (ROWS, LANES), 1)

    def block_rows(i):
        at, deep = slice(i * ROWS, (i + 1) * ROWS), slice((3 + i) * ROWS, (4 + i) * ROWS)
        coef, winds = east[at, :], field[at, COLS:]
        begin = field[at, 0:LANES] + jnp.where(tile_lane == 0, coef * from_left[at, :], 0.0)
        end = field[at, COLS - LANES : COLS] - jnp.where(tile_lane == LANES - 1, coef * from_right[at, :], 0.0)
        beyond = jnp.where(tile_lane < LANES // 2, from_right[at, :], from_left[at, :])
        beyond = beyond + jnp.where(tile_lane == 0, coef * pltpu.roll(winds, 1, 1), 0.0)
        beyond = beyond - jnp.where(tile_lane == LANES - 1, coef * pltpu.roll(winds, LANES - 1, 1), 0.0)
        rhs = jnp.concatenate([begin, field[at, LANES : COLS - LANES], end, beyond], axis=1)
        beyond = jnp.where(tile_lane < LANES // 2, from_right[deep, :], from_left[deep, :])
        return rhs, jnp.concatenate([depths[at, :], beyond], axis=1)

    parts = [block_rows(i) for i in range(3)]

    lane = lax.broadcasted_iota(jnp.int32, (ROWS, LANES), 1)
    sub = lax.broadcasted_iota(jnp.int32, (ROWS, LANES), 0)

    def owner(tile):
        return lax.rem(tile * LANES + lane, TILES)

    def dealt(wide, t):
        value = wide[:, 0:LANES]
        for q in range(1, TILES):
            value = jnp.where(owner(q) == t, wide[:, q * LANES : (q + 1) * LANES], value)
        return jnp.take_along_axis(value, lax.rem(lane * TILES + t, LANES), axis=1)

    for i, (rhs, deep) in enumerate(parts):
        at = slice(i * ROWS, (i + 1) * ROWS)
        z = zonal[at, :]
        for t in range(TILES):
            d = dealt(deep, t)
            rhs_w[t, at, :] = dealt(rhs, t) / d
            base_w[t, at, :] = coriolis[at, :] + 2.0 * d * (z + merid_coupling)
            if i == 0:
                d = jnp.where(top, 0.0, d)
            if i == 2:
                d = jnp.where(bottom, 0.0, d)
            depth_w[t, at, :] = d

    numbers = jnp.broadcast_to(one[...] + two[...], (ROWS, LANES))
    groups = POLES // ROWS
    for g in range(groups):
        for which in range(4):
            picked = jnp.where(lane == which * POLES + g * ROWS + sub, numbers, 0.0)
            poles[g, which] = jnp.broadcast_to(jnp.sum(picked, axis=1, keepdims=True), (ROWS, LANES))
    first, end = ROWS - HALO, 2 * ROWS + HALO

    def spread(ref, j, *index):
        return jnp.broadcast_to(ref[(*index, slice(j, j + 1), slice(None))], (ROWS, LANES))

    def begin(i, carry):
        g, t = i // TILES, lax.rem(i, TILES)
        real, imag = poles[g, 0], poles[g, 1]
        imag_sq = imag * imag
        for j in range(first, end):
            diag = real + spread(base_w, j, t)
            scale = spread(depth_w, j, t) / (diag * diag + imag_sq)
            g_real, g_imag = scale * diag, -(scale * imag)
            gain[g, 0, j, t] = g_real
            gain[g, 1, j, t] = g_imag
            r = spread(rhs_w, j, t)
            even_p[g, 0, j, t] = r * g_real
            even_p[g, 1, j, t] = r * g_imag
        return carry

    lax.fori_loop(0, groups * TILES, begin, 0)
    alpha = 1.0
    for m, w in enumerate(relax_weights):
        old, new = (even_p, odd_p) if m % 2 == 0 else (odd_p, even_p)
        low, high = first + m + 1, end - m - 1
        last = m == len(relax_weights) - 1

        def one_row(g, j):
            z = jnp.broadcast_to(zonal[pl.ds(j, 1), :], (ROWS, LANES))
            here = [[old[g, c, j, t] for t in range(TILES)] for c in range(2)]
            west = [pltpu.roll(here[c][TILES - 1], 1, 1) for c in range(2)]
            east = [pltpu.roll(here[c][0], LANES - 1, 1) for c in range(2)]
            for t in range(TILES):
                s_real, s_imag = (
                    z * ((here[c][t - 1] if t else west[c]) + (here[c][t + 1] if t < TILES - 1 else east[c]))
                    + (old[g, c, j - 1, t] + old[g, c, j + 1, t])
                    for c in range(2)
                )
                s_real = s_real + jnp.broadcast_to(rhs_w[t, pl.ds(j, 1), :], (ROWS, LANES))
                g_real, g_imag = gain[g, 0, j, t], gain[g, 1, j, t]
                u_real = s_real * g_real - s_imag * g_imag
                u_imag = s_real * g_imag + s_imag * g_real
                if w != 1.0:
                    u_real = u_real + ((1.0 - w) / w) * here[0][t]
                    u_imag = u_imag + ((1.0 - w) / w) * here[1][t]
                if last:
                    wreal, wimag = alpha * poles[g, 2], alpha * poles[g, 3]
                    value = jnp.sum(wreal * u_real - wimag * u_imag, axis=0, keepdims=True)
                    result[g, t, pl.ds(j - ROWS, 1), :] = value
                else:
                    new[g, 0, j, t] = u_real
                    new[g, 1, j, t] = u_imag

        def sweep(i, carry):
            for g in range(groups):
                for k in range(2):
                    one_row(g, low + 2 * i + k)
            return carry

        lax.fori_loop(0, (high - low) // 2, sweep, 0)
        if w != 1.0:
            alpha = alpha * w
            rhs_w[...] = rhs_w[...] * (1.0 / w)

    undealt = []
    for t in range(TILES):
        value = result[0, t]
        for g in range(1, groups):
            value = value + result[g, t]
        index = lax.rem((lane - t + LANES) * INVERSE, LANES)
        undealt.append(jnp.take_along_axis(value, index, axis=1))
    for q in range(COLS // LANES):
        value = undealt[0]
        for t in range(1, TILES):
            value = jnp.where(owner(q) == t, undealt[t], value)
        out[:, q * LANES : (q + 1) * LANES] = value


def shape(*dims):
    return jax.ShapeDtypeStruct(dims, F32)


def call(kernel, outs, n_in, flops, scratch=()):
    return pl.pallas_call(
        kernel,
        out_shape=outs,
        in_specs=[VMEM] * n_in,
        out_specs=[VMEM] * len(outs),
        scratch_shapes=list(scratch),
        cost_estimate=pl.CostEstimate(flops=flops, bytes_accessed=200000, transcendentals=0),
        compiler_params=pltpu.CompilerParams(vmem_limit_bytes=LIMIT),
    )


def body(height, east_wind, north_wind, depth, pole_real, pole_imag, weight_real, weight_imag):
    n_pole, n_lat, n_lon = (lax.axis_size(a) for a in ("pole", "lat", "lon"))

    pole = lax.axis_index("pole")
    at = lax.broadcasted_iota(jnp.int32, (1, LANES), 1)
    table = jnp.zeros((1, LANES), F32)
    for i, value in enumerate((pole_real, pole_imag, weight_real, weight_imag)):
        table = jnp.where(at == i * POLES + pole, value[0], table)
    layers = n_pole // 2

    def swapped(table, partner):
        pairs = [(2 * z + x, 2 * partner(z) + x) for z in range(layers) for x in range(2)]
        return lax.ppermute(table, "pole", pairs)

    one = table + swapped(table, lambda z: layers - 1 - z)
    two = swapped(one, lambda z: z ^ 2)

    wide, both = shape(ROWS, WIDE), shape(2 * ROWS, WIDE)
    send_near, send_far = pl.pallas_call(
        rows_kernel,
        out_shape=[wide, both],
        in_specs=[pl.BlockSpec(memory_space=pl.ANY)] * 4,
        out_specs=[VMEM] * 2,
        scratch_shapes=[pltpu.VMEM((4, ROWS, COLS), F32), pltpu.SemaphoreType.DMA((4,))],
        compiler_params=pltpu.CompilerParams(vmem_limit_bytes=66600000),
    )(height, east_wind, north_wind, depth)
    total = n_lat * n_pole
    far_pairs = []
    for r in range(1, total, 2):
        for c in range(n_lon):
            here, there = (((b % n_pole) * n_lat + b // n_pole) * n_lon + c for b in (r, (r + 1) % total))
            far_pairs += [(here, there), (there, here)]
    far = lax.ppermute(send_far, ("pole", "lat", "lon"), far_pairs)
    beside = [(i, i ^ 1) for i in range(n_pole)]
    near = lax.ppermute(send_near, "pole", beside)

    tall, terms, column = shape(3 * ROWS, COLS), shape(3 * ROWS, LANES), shape(6 * ROWS, LANES)
    field, depths, coriolis, zonal, east_coef, to_right, to_left = call(
        columns_kernel, [shape(3 * ROWS, WIDE), tall, terms, terms, terms, column, column], 6, 100000
    )(height, east_wind, north_wind, depth, near, far)
    from_left = lax.ppermute(to_right, "lon", [(i, (i + 1) % n_lon) for i in range(n_lon)])
    from_right = lax.ppermute(to_left, "lon", [((i + 1) % n_lon, i) for i in range(n_lon)])

    (one,) = pl.pallas_call(
        merge_kernel,
        out_shape=[shape(1, LANES)],
        in_specs=[VMEM, VMEM, pl.BlockSpec(memory_space=pl.ANY)],
        out_specs=[VMEM],
        compiler_params=pltpu.CompilerParams(vmem_limit_bytes=LIMIT),
    )(one, two, to_right)
    one = one + swapped(one, lambda z: z ^ 1)
    two = lax.ppermute(one, "pole", beside)

    groups = POLES // ROWS
    tiles = pltpu.VMEM((TILES, 3 * ROWS, LANES), F32)
    iterate = pltpu.VMEM((groups, 2, 3 * ROWS, TILES, ROWS, LANES), F32)
    scratch = [
        tiles,
        tiles,
        tiles,
        pltpu.VMEM((groups, 4, ROWS, LANES), F32),
        pltpu.VMEM((groups, 2, 3 * ROWS, TILES, ROWS, LANES), F32),
        iterate,
        iterate,
        pltpu.VMEM((groups, TILES, ROWS, LANES), F32),
    ]
    (out,) = call(solve_kernel, [shape(ROWS, COLS)], 9, 60000000, scratch)(
        field, depths, from_left, from_right, one, two, coriolis, zonal, east_coef
    )
    return out


def solution(mesh):
    rows = P(("lat", "pole"), "lon")
    one = P("pole")
    in_specs = (rows, rows, rows, P("lat", "lon"), one, one, one, one)
    return jax.shard_map(body, mesh=mesh, in_specs=in_specs, out_specs=rows, check_vma=False)
```

```python
import functools
import math

import jax
import jax.numpy as jnp
from jax import lax
from jax.experimental import pallas as pl
from jax.experimental.pallas import tpu as pltpu
from jax.sharding import PartitionSpec as P

coriolis_max = 1.0
zonal_coupling = 1.0
merid_coupling = 1.0
flux_scale = 0.5
north_scale = 0.25
relax_weights = (0.8, 1.0, 0.9, 1.0, 0.85, 1.0)

POLES = 16
LANES = 128
ROWS = 8
COLS = 1024
HALO = 6
TILES = 9
WIDE = TILES * LANES
INVERSE = pow(TILES, -1, LANES)
F32 = jnp.float32
LIMIT = 24 * 1024 * 1024

VMEM = pl.BlockSpec(memory_space=pltpu.VMEM)


def row_terms(row_index, total_rows):
    theta = math.pi * ((row_index + 0.5) / total_rows - 0.5)
    cosine = jnp.cos(theta)
    coriolis = coriolis_max * jnp.sin(theta)
    coriolis_sq = coriolis * coriolis
    zonal_coef = zonal_coupling / (cosine * cosine + 0.01)
    east_coef = flux_scale / (cosine + 0.05)
    return coriolis_sq, zonal_coef, east_coef


def near_depth(depth_at, block, depth_rows, columns):
    last = depth_rows // ROWS - 1
    rows = [jnp.maximum(block - 1, 0), block, jnp.minimum(block + 1, last)]
    return [depth_at[pl.ds(pl.multiple_of(r * ROWS, ROWS), ROWS), columns] for r in rows]


def edges_kernel(height, east, north, depth, to_right, to_left, around, sems):
    block = lax.axis_index("pole")
    copies = []
    for out, first in ((to_right, COLS - LANES), (to_left, 0)):
        columns = pl.ds(first, LANES)
        parts = [height.at[:, columns], east.at[:, columns], north.at[:, columns]]
        parts += near_depth(depth.at, block, depth.shape[0], columns)
        copies += [(part, out.at[pl.ds(i * ROWS, ROWS), :]) for i, part in enumerate(parts)]
    parts = near_depth(depth.at, block, depth.shape[0], pl.ds(0, COLS))
    copies += [(part, around.at[pl.ds(i * ROWS, ROWS), :]) for i, part in enumerate(parts)]
    copies = [pltpu.make_async_copy(source, target, sems.at[i]) for i, (source, target) in enumerate(copies)]
    for copy in copies:
        copy.start()
    for copy in copies:
        copy.wait()


def near_kernel(rows, one, two, out):
    out[0 : ROWS - 1, :] = rows[0 : ROWS - 1, :]
    out[ROWS - 1 : ROWS, 0:LANES] = one[...] + two[...]
    out[ROWS - 1 : ROWS, LANES:] = rows[ROWS - 1 : ROWS, LANES:]


def rows_kernel(height, east, north, around, from_left, from_right, after, field, winds, depths, send_near, send_far, coriolis, zonal):
    block, band = lax.axis_index("pole"), lax.axis_index("lat")
    total_rows = lax.axis_size("lat") * lax.axis_size("pole") * ROWS
    first_row = (band * lax.axis_size("pole") + block) * ROWS - ROWS
    index = (first_row + lax.broadcasted_iota(jnp.int32, (3 * ROWS, LANES), 0)).astype(F32)
    coriolis[...], zonal[...], east_coef = row_terms(index, total_rows)
    east_coef = east_coef[ROWS : 2 * ROWS, :]
    even = lax.rem(block, 2) == 0
    lane = lax.broadcasted_iota(jnp.int32, (ROWS, LANES), 1)
    row = lax.broadcasted_iota(jnp.int32, (ROWS, WIDE), 0)

    def widened(own, part):
        at = slice(part * ROWS, (part + 1) * ROWS)
        return jnp.concatenate([own, jnp.where(lane < LANES // 2, from_right[at, :], from_left[at, :])], axis=1)

    high = widened(height[...], 0)
    eastward = widened(east[...], 1)
    northward = widened(north[...], 2)
    coef = jnp.concatenate([east_coef] * TILES, axis=1)
    partial = high - coef * (pltpu.roll(eastward, WIDE - 1, 1) - pltpu.roll(eastward, 1, 1))
    below = jnp.where(row == ROWS - 1, 0.0, pltpu.roll(northward, ROWS - 1, 0))
    above = jnp.where(row == 0, 0.0, pltpu.roll(northward, 1, 0))
    partial = partial - north_scale * (below - above)
    field[...] = partial
    winds[...] = northward
    upward = jnp.where(row < HALO, partial, pltpu.roll(northward, HALO, 0))
    downward = jnp.where(row < HALO, pltpu.roll(partial, ROWS - 2, 0), pltpu.roll(northward, ROWS - 1, 0))
    send_near[...] = jnp.where(even, downward, upward)
    send_far[0:ROWS, :] = jnp.where(even, upward, downward)
    for i in range(3):
        part = widened(around[i * ROWS : (i + 1) * ROWS, :], 3 + i)
        depths[i * ROWS : (i + 1) * ROWS, :] = part
        if i == 1:
            send_far[ROWS : 2 * ROWS, :] = part


def solve_kernel(field, winds, depths, near, far, one, two, coriolis, zonal, out, rhs_w, depth_w, base_w, poles, gain, even_p, odd_p, result):
    block = lax.axis_index("pole")
    band = lax.axis_index("lat")
    even = lax.rem(block, 2) == 0
    top = jnp.logical_and(band == 0, block == 0)
    last_block = lax.axis_size("pole") - 1
    bottom = jnp.logical_and(band == lax.axis_size("lat") - 1, block == last_block)
    row = lax.broadcasted_iota(jnp.int32, (ROWS, WIDE), 0)

    near_rows, far_rows, far_depth = near[...], far[0:ROWS, :], far[ROWS : 2 * ROWS, :]
    upper = jnp.where(top, 0.0, jnp.where(even, far_rows, near_rows))
    lower = jnp.where(bottom, 0.0, jnp.where(even, near_rows, far_rows))
    north = winds[...]
    from_above = north_scale * pltpu.roll(upper, ROWS - HALO, 0)
    from_below = north_scale * pltpu.roll(lower, 1, 0)
    mid = field[...] + jnp.where(row == 0, from_above, 0.0) - jnp.where(row == ROWS - 1, from_below, 0.0)
    own_first = jnp.where(top, 0.0, north_scale * pltpu.roll(north, ROWS - 1, 0))
    own_last = jnp.where(bottom, 0.0, north_scale * pltpu.roll(north, 1, 0))
    above = pltpu.roll(upper, ROWS - HALO, 0) - jnp.where(row == ROWS - 1, own_first, 0.0)
    below = lower + jnp.where(row == 0, own_last, 0.0)
    d_above = jnp.where(block == 0, far_depth, depths[0:ROWS, :])
    d_mid = depths[ROWS : 2 * ROWS, :]
    d_below = jnp.where(block == last_block, far_depth, depths[2 * ROWS : 3 * ROWS, :])

    lane = lax.broadcasted_iota(jnp.int32, (ROWS, LANES), 1)
    sub = lax.broadcasted_iota(jnp.int32, (ROWS, LANES), 0)

    def owner(tile):
        return lax.rem(tile * LANES + lane, TILES)

    def dealt(wide, t):
        value = wide[:, 0:LANES]
        for q in range(1, TILES):
            value = jnp.where(owner(q) == t, wide[:, q * LANES : (q + 1) * LANES], value)
        return jnp.take_along_axis(value, lax.rem(lane * TILES + t, LANES), axis=1)

    for i, (rhs, deep) in enumerate(((above, d_above), (mid, d_mid), (below, d_below))):
        at = slice(i * ROWS, (i + 1) * ROWS)
        z = zonal[at, :]
        for t in range(TILES):
            d = dealt(deep, t)
            rhs_w[t, at, :] = dealt(rhs, t) / d
            base_w[t, at, :] = coriolis[at, :] + 2.0 * d * (z + merid_coupling)
            if i == 0:
                d = jnp.where(top, 0.0, d)
            if i == 2:
                d = jnp.where(bottom, 0.0, d)
            depth_w[t, at, :] = d

    numbers = jnp.broadcast_to((one[...] + two[...]) + near[ROWS - 1 : ROWS, 0:LANES], (ROWS, LANES))
    groups = POLES // ROWS
    for g in range(groups):
        for which in range(4):
            picked = jnp.where(lane == which * POLES + g * ROWS + sub, numbers, 0.0)
            poles[g, which] = jnp.broadcast_to(jnp.sum(picked, axis=1, keepdims=True), (ROWS, LANES))
    first, end = ROWS - HALO, 2 * ROWS + HALO

    def spread(ref, j, *index):
        return jnp.broadcast_to(ref[(*index, slice(j, j + 1), slice(None))], (ROWS, LANES))

    def begin(i, carry):
        g, t = i // TILES, lax.rem(i, TILES)
        real, imag = poles[g, 0], poles[g, 1]
        imag_sq = imag * imag
        for j in range(first, end):
            diag = real + spread(base_w, j, t)
            scale = spread(depth_w, j, t) / (diag * diag + imag_sq)
            g_real, g_imag = scale * diag, -(scale * imag)
            gain[g, 0, j, t] = g_real
            gain[g, 1, j, t] = g_imag
            r = spread(rhs_w, j, t)
            even_p[g, 0, j, t] = r * g_real
            even_p[g, 1, j, t] = r * g_imag
        return carry

    lax.fori_loop(0, groups * TILES, begin, 0)
    alpha = 1.0
    for m, w in enumerate(relax_weights):
        old, new = (even_p, odd_p) if m % 2 == 0 else (odd_p, even_p)
        low, high = first + m + 1, end - m - 1
        last = m == len(relax_weights) - 1

        def one_row(g, j):
            weighted = []
            z = jnp.broadcast_to(zonal[pl.ds(j, 1), :], (ROWS, LANES))
            here = [[old[g, c, j, t] for t in range(TILES)] for c in range(2)]
            west = [pltpu.roll(here[c][TILES - 1], 1, 1) for c in range(2)]
            east = [pltpu.roll(here[c][0], LANES - 1, 1) for c in range(2)]
            for t in range(TILES):
                s_real, s_imag = (
                    z * ((here[c][t - 1] if t else west[c]) + (here[c][t + 1] if t < TILES - 1 else east[c]))
                    + (old[g, c, j - 1, t] + old[g, c, j + 1, t])
                    for c in range(2)
                )
                s_real = s_real + jnp.broadcast_to(rhs_w[t, pl.ds(j, 1), :], (ROWS, LANES))
                g_real, g_imag = gain[g, 0, j, t], gain[g, 1, j, t]
                u_real = s_real * g_real - s_imag * g_imag
                u_imag = s_real * g_imag + s_imag * g_real
                if w != 1.0:
                    u_real = u_real + ((1.0 - w) / w) * here[0][t]
                    u_imag = u_imag + ((1.0 - w) / w) * here[1][t]
                if last:
                    weighted.append(weights[g][0] * u_real - weights[g][1] * u_imag)
                else:
                    new[g, 0, j, t] = u_real
                    new[g, 1, j, t] = u_imag
            return weighted

        if last:
            weights = [[alpha * poles[g, which] for which in (2, 3)] for g in range(groups)]
        for j in range(low, high):
            weighted = [one_row(g, j) for g in range(groups)]
            for t in range(TILES if last else 0):
                value = functools.reduce(jnp.add, [of_group[t] for of_group in weighted])
                result[t, j - ROWS : j - ROWS + 1, :] = jnp.sum(value, axis=0, keepdims=True)
        if w != 1.0:
            alpha = alpha * w
            rhs_w[...] = rhs_w[...] * (1.0 / w)

    undealt = []
    for t in range(TILES):
        index = lax.rem((lane - t + LANES) * INVERSE, LANES)
        undealt.append(jnp.take_along_axis(result[t], index, axis=1))
    for q in range(COLS // LANES):
        value = undealt[0]
        for t in range(1, TILES):
            value = jnp.where(owner(q) == t, undealt[t], value)
        out[:, q * LANES : (q + 1) * LANES] = value


def shape(*dims):
    return jax.ShapeDtypeStruct(dims, F32)


def call(kernel, outs, n_in, flops, scratch=()):
    return pl.pallas_call(
        kernel,
        out_shape=outs,
        in_specs=[VMEM] * n_in,
        out_specs=[VMEM] * len(outs),
        scratch_shapes=list(scratch),
        cost_estimate=pl.CostEstimate(flops=flops, bytes_accessed=200000, transcendentals=0),
        compiler_params=pltpu.CompilerParams(vmem_limit_bytes=LIMIT),
    )


def body(height, east_wind, north_wind, depth, pole_real, pole_imag, weight_real, weight_imag):
    n_pole, n_lat, n_lon = (lax.axis_size(a) for a in ("pole", "lat", "lon"))
    pole = lax.axis_index("pole")
    at = lax.broadcasted_iota(jnp.int32, (1, LANES), 1)
    table = jnp.zeros((1, LANES), F32)
    for i, value in enumerate((pole_real, pole_imag, weight_real, weight_imag)):
        table = jnp.where(at == i * POLES + pole, value[0], table)
    layers = n_pole // 2

    def swapped(table, partner):
        pairs = [(2 * z + x, 2 * partner(z) + x) for z in range(layers) for x in range(2)]
        return lax.ppermute(table, "pole", pairs)

    table = first = (table + swapped(table, lambda z: layers - 1 - z))[0:1]
    table = table + swapped(table, lambda z: z ^ 2)
    third = swapped(table, lambda z: z ^ 1)

    column = shape(6 * ROWS, LANES)
    to_right, to_left, around = pl.pallas_call(
        edges_kernel,
        out_shape=[column, column, shape(3 * ROWS, COLS)],
        in_specs=[pl.BlockSpec(memory_space=pl.ANY)] * 4,
        out_specs=[VMEM] * 3,
        scratch_shapes=[pltpu.SemaphoreType.DMA((15,))],
        compiler_params=pltpu.CompilerParams(vmem_limit_bytes=66600000),
    )(height, east_wind, north_wind, depth)
    from_left = lax.ppermute(to_right, "lon", [(i, (i + 1) % n_lon) for i in range(n_lon)])
    from_right = lax.ppermute(to_left, "lon", [((i + 1) % n_lon, i) for i in range(n_lon)])
    wide, both = shape(ROWS, WIDE), shape(2 * ROWS, WIDE)
    terms = shape(3 * ROWS, LANES)
    field, winds, depths, send_near, send_far, coriolis, zonal = call(
        rows_kernel, [wide, wide, shape(3 * ROWS, WIDE), wide, both, terms, terms], 7, 100000
    )(height, east_wind, north_wind, around, from_left, from_right, first)

    total = n_lat * n_pole
    far_pairs = []
    for r in range(1, total, 2):
        for c in range(n_lon):
            one, two = (((b % n_pole) * n_lat + b // n_pole) * n_lon + c for b in (r, (r + 1) % total))
            far_pairs += [(one, two), (two, one)]
    far = lax.ppermute(send_far, ("pole", "lat", "lon"), far_pairs)
    (send_near,) = pl.pallas_call(
        near_kernel,
        out_shape=[wide],
        in_specs=[VMEM, VMEM, VMEM],
        out_specs=[VMEM],
        compiler_params=pltpu.CompilerParams(vmem_limit_bytes=LIMIT),
    )(send_near, table, third)
    near = lax.ppermute(send_near, "pole", [(i, i ^ 1) for i in range(n_pole)])

    groups = POLES // ROWS
    tiles = pltpu.VMEM((TILES, 3 * ROWS, LANES), F32)
    iterate = pltpu.VMEM((groups, 2, 3 * ROWS, TILES, ROWS, LANES), F32)
    scratch = [
        tiles,
        tiles,
        tiles,
        pltpu.VMEM((groups, 4, ROWS, LANES), F32),
        pltpu.VMEM((groups, 2, 3 * ROWS, TILES, ROWS, LANES), F32),
        iterate,
        iterate,
        pltpu.VMEM((TILES, ROWS, LANES), F32),
    ]
    (out,) = call(solve_kernel, [shape(ROWS, COLS)], 9, 60000000, scratch)(
        field, winds, depths, near, far, table, third, coriolis, zonal
    )
    return out


def solution(mesh):
    rows = P(("lat", "pole"), "lon")
    one = P("pole")
    in_specs = (rows, rows, rows, P("lat", "lon"), one, one, one, one)
    return jax.shard_map(body, mesh=mesh, in_specs=in_specs, out_specs=rows, check_vma=False)
```

```python
import functools
import math

import jax
import jax.numpy as jnp
from jax import lax
from jax.experimental import pallas as pl
from jax.experimental.pallas import tpu as pltpu
from jax.sharding import PartitionSpec as P

coriolis_max = 1.0
zonal_coupling = 1.0
merid_coupling = 1.0
flux_scale = 0.5
north_scale = 0.25
relax_weights = (0.8, 1.0, 0.9, 1.0, 0.85, 1.0)

POLES = 16
LANES = 128
ROWS = 8
COLS = 1024
HALO = 6
TILES = 9
WIDE = TILES * LANES
INVERSE = pow(TILES, -1, LANES)
F32 = jnp.float32
LIMIT = 24 * 1024 * 1024

VMEM = pl.BlockSpec(memory_space=pltpu.VMEM)


def row_terms(row_index, total_rows):
    theta = math.pi * ((row_index + 0.5) / total_rows - 0.5)
    cosine = jnp.cos(theta)
    coriolis = coriolis_max * jnp.sin(theta)
    coriolis_sq = coriolis * coriolis
    zonal_coef = zonal_coupling / (cosine * cosine + 0.01)
    east_coef = flux_scale / (cosine + 0.05)
    return coriolis_sq, zonal_coef, east_coef


def near_depth(depth_at, block, depth_rows, columns):
    last = depth_rows // ROWS - 1
    rows = [jnp.maximum(block - 1, 0), block, jnp.minimum(block + 1, last)]
    return [depth_at[pl.ds(pl.multiple_of(r * ROWS, ROWS), ROWS), columns] for r in rows]


def edges_kernel(height, east, north, depth, to_right, to_left, sems):
    block = lax.axis_index("pole")
    copies = []
    for out, first in ((to_right, COLS - LANES), (to_left, 0)):
        columns = pl.ds(first, LANES)
        parts = [height.at[:, columns], east.at[:, columns], north.at[:, columns]]
        parts += near_depth(depth.at, block, depth.shape[0], columns)
        copies += [(part, out.at[pl.ds(i * ROWS, ROWS), :]) for i, part in enumerate(parts)]
    copies = [pltpu.make_async_copy(source, target, sems.at[i]) for i, (source, target) in enumerate(copies)]
    for copy in copies:
        copy.start()
    for copy in copies:
        copy.wait()


def near_kernel(rows, one, two, out):
    out[0 : ROWS - 1, :] = rows[0 : ROWS - 1, :]
    out[ROWS - 1 : ROWS, 0:LANES] = one[...] + two[...]
    out[ROWS - 1 : ROWS, LANES:] = rows[ROWS - 1 : ROWS, LANES:]


def rows_kernel(height, east, north, around, from_left, from_right, after, field, winds, depths, send_near, send_far, coriolis, zonal):
    block, band = lax.axis_index("pole"), lax.axis_index("lat")
    total_rows = lax.axis_size("lat") * lax.axis_size("pole") * ROWS
    first_row = (band * lax.axis_size("pole") + block) * ROWS - ROWS
    index = (first_row + lax.broadcasted_iota(jnp.int32, (3 * ROWS, LANES), 0)).astype(F32)
    coriolis[...], zonal[...], east_coef = row_terms(index, total_rows)
    east_coef = east_coef[ROWS : 2 * ROWS, :]
    even = lax.rem(block, 2) == 0
    lane = lax.broadcasted_iota(jnp.int32, (ROWS, LANES), 1)
    row = lax.broadcasted_iota(jnp.int32, (ROWS, WIDE), 0)

    def widened(own, part):
        at = slice(part * ROWS, (part + 1) * ROWS)
        return jnp.concatenate([own, jnp.where(lane < LANES // 2, from_right[at, :], from_left[at, :])], axis=1)

    high = widened(height[...], 0)
    eastward = widened(east[...], 1)
    northward = widened(north[...], 2)
    coef = jnp.concatenate([east_coef] * TILES, axis=1)
    partial = high - coef * (pltpu.roll(eastward, WIDE - 1, 1) - pltpu.roll(eastward, 1, 1))
    below = jnp.where(row == ROWS - 1, 0.0, pltpu.roll(northward, ROWS - 1, 0))
    above = jnp.where(row == 0, 0.0, pltpu.roll(northward, 1, 0))
    partial = partial - north_scale * (below - above)
    field[...] = partial
    winds[...] = northward
    upward = jnp.where(row < HALO, partial, pltpu.roll(northward, HALO, 0))
    downward = jnp.where(row < HALO, pltpu.roll(partial, ROWS - 2, 0), pltpu.roll(northward, ROWS - 1, 0))
    send_near[...] = jnp.where(even, downward, upward)
    send_far[0:ROWS, :] = jnp.where(even, upward, downward)
    for i in range(3):
        part = widened(around[i * ROWS : (i + 1) * ROWS, :], 3 + i)
        depths[i * ROWS : (i + 1) * ROWS, :] = part
        if i == 1:
            send_far[ROWS : 2 * ROWS, :] = part


def solve_kernel(field, winds, depths, near, far, one, two, coriolis, zonal, out, rhs_w, depth_w, base_w, poles, gain, even_p, odd_p, result):
    block = lax.axis_index("pole")
    band = lax.axis_index("lat")
    even = lax.rem(block, 2) == 0
    top = jnp.logical_and(band == 0, block == 0)
    last_block = lax.axis_size("pole") - 1
    bottom = jnp.logical_and(band == lax.axis_size("lat") - 1, block == last_block)
    row = lax.broadcasted_iota(jnp.int32, (ROWS, WIDE), 0)

    near_rows, far_rows, far_depth = near[...], far[0:ROWS, :], far[ROWS : 2 * ROWS, :]
    upper = jnp.where(top, 0.0, jnp.where(even, far_rows, near_rows))
    lower = jnp.where(bottom, 0.0, jnp.where(even, near_rows, far_rows))
    north = winds[...]
    from_above = north_scale * pltpu.roll(upper, ROWS - HALO, 0)
    from_below = north_scale * pltpu.roll(lower, 1, 0)
    mid = field[...] + jnp.where(row == 0, from_above, 0.0) - jnp.where(row == ROWS - 1, from_below, 0.0)
    own_first = jnp.where(top, 0.0, north_scale * pltpu.roll(north, ROWS - 1, 0))
    own_last = jnp.where(bottom, 0.0, north_scale * pltpu.roll(north, 1, 0))
    above = pltpu.roll(upper, ROWS - HALO, 0) - jnp.where(row == ROWS - 1, own_first, 0.0)
    below = lower + jnp.where(row == 0, own_last, 0.0)
    d_above = jnp.where(block == 0, far_depth, depths[0:ROWS, :])
    d_mid = depths[ROWS : 2 * ROWS, :]
    d_below = jnp.where(block == last_block, far_depth, depths[2 * ROWS : 3 * ROWS, :])

    lane = lax.broadcasted_iota(jnp.int32, (ROWS, LANES), 1)
    sub = lax.broadcasted_iota(jnp.int32, (ROWS, LANES), 0)

    def owner(tile):
        return lax.rem(tile * LANES + lane, TILES)

    def dealt(wide, t):
        value = wide[:, 0:LANES]
        for q in range(1, TILES):
            value = jnp.where(owner(q) == t, wide[:, q * LANES : (q + 1) * LANES], value)
        return jnp.take_along_axis(value, lax.rem(lane * TILES + t, LANES), axis=1)

    for i, (rhs, deep) in enumerate(((above, d_above), (mid, d_mid), (below, d_below))):
        at = slice(i * ROWS, (i + 1) * ROWS)
        z = zonal[at, :]
        for t in range(TILES):
            d = dealt(deep, t)
            rhs_w[t, at, :] = dealt(rhs, t) / d
            base_w[t, at, :] = coriolis[at, :] + 2.0 * d * (z + merid_coupling)
            if i == 0:
                d = jnp.where(top, 0.0, d)
            if i == 2:
                d = jnp.where(bottom, 0.0, d)
            depth_w[t, at, :] = d

    numbers = jnp.broadcast_to((one[...] + two[...]) + near[ROWS - 1 : ROWS, 0:LANES], (ROWS, LANES))
    groups = POLES // ROWS
    for g in range(groups):
        for which in range(4):
            picked = jnp.where(lane == which * POLES + g * ROWS + sub, numbers, 0.0)
            poles[g, which] = jnp.broadcast_to(jnp.sum(picked, axis=1, keepdims=True), (ROWS, LANES))
    first, end = ROWS - HALO, 2 * ROWS + HALO

    def spread(ref, j, *index):
        return jnp.broadcast_to(ref[(*index, slice(j, j + 1), slice(None))], (ROWS, LANES))

    def begin(i, carry):
        g, t = i // TILES, lax.rem(i, TILES)
        real, imag = poles[g, 0], poles[g, 1]
        imag_sq = imag * imag
        for j in range(first, end):
            diag = real + spread(base_w, j, t)
            scale = spread(depth_w, j, t) / (diag * diag + imag_sq)
            g_real, g_imag = scale * diag, -(scale * imag)
            gain[g, 0, j, t] = g_real
            gain[g, 1, j, t] = g_imag
            r = spread(rhs_w, j, t)
            even_p[g, 0, j, t] = r * g_real
            even_p[g, 1, j, t] = r * g_imag
        return carry

    lax.fori_loop(0, groups * TILES, begin, 0)
    alpha = 1.0
    for m, w in enumerate(relax_weights):
        old, new = (even_p, odd_p) if m % 2 == 0 else (odd_p, even_p)
        low, high = first + m + 1, end - m - 1
        last = m == len(relax_weights) - 1

        def one_row(g, j):
            weighted = []
            z = jnp.broadcast_to(zonal[pl.ds(j, 1), :], (ROWS, LANES))
            here = [[old[g, c, j, t] for t in range(TILES)] for c in range(2)]
            west = [pltpu.roll(here[c][TILES - 1], 1, 1) for c in range(2)]
            east = [pltpu.roll(here[c][0], LANES - 1, 1) for c in range(2)]
            for t in range(TILES):
                s_real, s_imag = (
                    z * ((here[c][t - 1] if t else west[c]) + (here[c][t + 1] if t < TILES - 1 else east[c]))
                    + (old[g, c, j - 1, t] + old[g, c, j + 1, t])
                    for c in range(2)
                )
                s_real = s_real + jnp.broadcast_to(rhs_w[t, pl.ds(j, 1), :], (ROWS, LANES))
                g_real, g_imag = gain[g, 0, j, t], gain[g, 1, j, t]
                u_real = s_real * g_real - s_imag * g_imag
                u_imag = s_real * g_imag + s_imag * g_real
                if w != 1.0:
                    u_real = u_real + ((1.0 - w) / w) * here[0][t]
                    u_imag = u_imag + ((1.0 - w) / w) * here[1][t]
                if last:
                    weighted.append(weights[g][0] * u_real - weights[g][1] * u_imag)
                else:
                    new[g, 0, j, t] = u_real
                    new[g, 1, j, t] = u_imag
            return weighted

        if last:
            weights = [[alpha * poles[g, which] for which in (2, 3)] for g in range(groups)]
        for j in range(low, high):
            weighted = [one_row(g, j) for g in range(groups)]
            for t in range(TILES if last else 0):
                value = functools.reduce(jnp.add, [of_group[t] for of_group in weighted])
                result[t, j - ROWS : j - ROWS + 1, :] = jnp.sum(value, axis=0, keepdims=True)
        if w != 1.0:
            alpha = alpha * w
            rhs_w[...] = rhs_w[...] * (1.0 / w)

    undealt = []
    for t in range(TILES):
        index = lax.rem((lane - t + LANES) * INVERSE, LANES)
        undealt.append(jnp.take_along_axis(result[t], index, axis=1))
    for q in range(COLS // LANES):
        value = undealt[0]
        for t in range(1, TILES):
            value = jnp.where(owner(q) == t, undealt[t], value)
        out[:, q * LANES : (q + 1) * LANES] = value


def shape(*dims):
    return jax.ShapeDtypeStruct(dims, F32)


def call(kernel, outs, n_in, flops, scratch=()):
    return pl.pallas_call(
        kernel,
        out_shape=outs,
        in_specs=[VMEM] * n_in,
        out_specs=[VMEM] * len(outs),
        scratch_shapes=list(scratch),
        cost_estimate=pl.CostEstimate(flops=flops, bytes_accessed=200000, transcendentals=0),
        compiler_params=pltpu.CompilerParams(vmem_limit_bytes=LIMIT),
    )


def body(height, east_wind, north_wind, depth, pole_real, pole_imag, weight_real, weight_imag):
    n_pole, n_lat, n_lon = (lax.axis_size(a) for a in ("pole", "lat", "lon"))
    pole = lax.axis_index("pole")
    at = lax.broadcasted_iota(jnp.int32, (1, LANES), 1)
    table = jnp.zeros((1, LANES), F32)
    for i, value in enumerate((pole_real, pole_imag, weight_real, weight_imag)):
        table = jnp.where(at == i * POLES + pole, value[0], table)
    layers = n_pole // 2

    def swapped(table, partner):
        pairs = [(2 * z + x, 2 * partner(z) + x) for z in range(layers) for x in range(2)]
        return lax.ppermute(table, "pole", pairs)

    table = first = (table + swapped(table, lambda z: layers - 1 - z))[0:1]
    table = table + swapped(table, lambda z: z ^ 2)
    third = swapped(table, lambda z: z ^ 1)

    blocks = [jnp.maximum(pole - 1, 0), pole, jnp.minimum(pole + 1, n_pole - 1)]
    around = jnp.concatenate([lax.dynamic_slice_in_dim(depth, b * ROWS, ROWS, 0) for b in blocks])

    column = shape(6 * ROWS, LANES)
    to_right, to_left = pl.pallas_call(
        edges_kernel,
        out_shape=[column, column],
        in_specs=[pl.BlockSpec(memory_space=pl.ANY)] * 4,
        out_specs=[VMEM] * 2,
        scratch_shapes=[pltpu.SemaphoreType.DMA((12,))],
        compiler_params=pltpu.CompilerParams(vmem_limit_bytes=66600000),
    )(height, east_wind, north_wind, depth)
    from_left = lax.ppermute(to_right, "lon", [(i, (i + 1) % n_lon) for i in range(n_lon)])
    from_right = lax.ppermute(to_left, "lon", [((i + 1) % n_lon, i) for i in range(n_lon)])
    wide, both = shape(ROWS, WIDE), shape(2 * ROWS, WIDE)
    terms = shape(3 * ROWS, LANES)
    field, winds, depths, send_near, send_far, coriolis, zonal = call(
        rows_kernel, [wide, wide, shape(3 * ROWS, WIDE), wide, both, terms, terms], 7, 100000
    )(height, east_wind, north_wind, around, from_left, from_right, first)

    total = n_lat * n_pole
    far_pairs = []
    for r in range(1, total, 2):
        for c in range(n_lon):
            one, two = (((b % n_pole) * n_lat + b // n_pole) * n_lon + c for b in (r, (r + 1) % total))
            far_pairs += [(one, two), (two, one)]
    far = lax.ppermute(send_far, ("pole", "lat", "lon"), far_pairs)
    (send_near,) = pl.pallas_call(
        near_kernel,
        out_shape=[wide],
        in_specs=[VMEM, VMEM, VMEM],
        out_specs=[VMEM],
        compiler_params=pltpu.CompilerParams(vmem_limit_bytes=LIMIT),
    )(send_near, table, third)
    near = lax.ppermute(send_near, "pole", [(i, i ^ 1) for i in range(n_pole)])

    groups = POLES // ROWS
    tiles = pltpu.VMEM((TILES, 3 * ROWS, LANES), F32)
    iterate = pltpu.VMEM((groups, 2, 3 * ROWS, TILES, ROWS, LANES), F32)
    scratch = [
        tiles,
        tiles,
        tiles,
        pltpu.VMEM((groups, 4, ROWS, LANES), F32),
        pltpu.VMEM((groups, 2, 3 * ROWS, TILES, ROWS, LANES), F32),
        iterate,
        iterate,
        pltpu.VMEM((TILES, ROWS, LANES), F32),
    ]
    (out,) = call(solve_kernel, [shape(ROWS, COLS)], 9, 60000000, scratch)(
        field, winds, depths, near, far, table, third, coriolis, zonal
    )
    return out


def solution(mesh):
    rows = P(("lat", "pole"), "lon")
    one = P("pole")
    in_specs = (rows, rows, rows, P("lat", "lon"), one, one, one, one)
    return jax.shard_map(body, mesh=mesh, in_specs=in_specs, out_specs=rows, check_vma=False)
```
